32 devices in a mesh: groups: 2 (over x), row: 16 (over z, y, core).
Axes of the slice: x: 2, y: 2, z: 4, core: 2. Of those that a mesh axis runs over, the one named last changes fastest.
Arguments:
- orbitals: bfloat16 [4096, 512], P(('groups', 'row')), parts along dimension 0, may hold values from -1.296875 to 1.296875
- basis: bfloat16 [4096, 1024], P(('groups', 'row')), parts along dimension 0, may hold values from -0.1875 to 0.1875
- kernel: bfloat16 [4096, 2048], P(('groups', 'row')), parts along dimension 0, may hold values from -6 to 6
Outputs:
- exchange_matrix: float32 [2048, 1024], P('groups', 'row'), parts along dimension 0
The draws below stay inside these ranges and needn't reach their ends.
There are 2 independent parts, one for each index of `groups`. The reference program is written for one: setup_inputs(seed, part) draws one part's arguments, and reference() takes and returns one part's arrays. A program takes and returns all parts, laid end to end along the dimension named above; each array names one. Nothing has to cross between parts.
All inputs are finite; a program needn't handle non-finite values.
Results may differ from the reference program's by a relative error of at most 0.0041.
Values may be sent and summed in bfloat16 or wider, within the bound.
No kernel may reach another device: no remote copies, remote signals or barrier semaphores. Data moves between devices by JAX's collectives and lax.ppermute only.
A program may use at most 128 MiB of HBM per device.

```python
import jax
import jax.numpy as jnp
from jax import lax

NOCC = 512
NB = 1024
NP = 2048


def spiked(entries, stream_key, source, target, parts, factor):
    owner, partner = [(jnp.arange(entries.shape[axis_at]) // (entries.shape[axis_at] // parts)).reshape([-1 if axis == axis_at else 1 for axis in range(entries.ndim)]) for axis_at in (source, target)]
    chosen = jax.random.permutation(stream_key, parts)[partner]
    strong = (owner == chosen) | (owner == (partner + parts // 2) % parts)
    return jnp.where(strong, factor * entries, entries)


def steps_of(own_key, shape, split, smallest, high):
    def one(dim, parts):
        draws = jax.random.uniform(jax.random.fold_in(jax.random.fold_in(own_key, 6), dim), (parts,), jnp.float32, smallest / len(split), high / len(split))
        return jnp.repeat(jnp.exp(draws), shape[dim] // parts).reshape((-1,) + (1,) * (len(shape) - dim - 1))

    loudness = one(*split[0])
    for cut in split[1:]:
        loudness = loudness * one(*cut)
    return loudness


def noise(stream_key, shape, spread, most, shards=(), kind=jnp.bfloat16):
    drawn = spread * jax.random.normal(stream_key, shape, jnp.float32)
    if shards:
        drawn = drawn * steps_of(stream_key, shape, shards, -0.22, 0.18)
    return jnp.clip(drawn, -most, most).astype(kind)


def noise_with(stream_key, extent, scale, reach, cuts, heavy, held_as=jnp.bfloat16):
    result = scale * jax.random.normal(stream_key, extent, jnp.float32)
    if cuts:
        result = result * steps_of(stream_key, extent, cuts, -0.22, 0.18)
    return jnp.clip(spiked(result, jax.random.fold_in(stream_key, 3), *heavy), -reach, reach).astype(held_as)


def setup_inputs(seed: int = 0, part: int = 0) -> dict:
    streams_of = jax.random.split(jax.random.key(seed), 4)
    part_splits = jax.random.split(jax.random.fold_in(streams_of[3], part), 4)
    return {
        "orbitals": noise(part_splits[0], (NP, NOCC), 0.21, 1.296875, ((0, 16),)),
        "basis": noise_with(part_splits[1], (NP, NB), NP ** -0.5, 0.1875, ((0, 16),), (0, 1, 16, 2.0)),
        "kernel": noise(part_splits[2], (NP, NP), 1.0, 6.0, ((0, 16),)),
    }


def reference(orbitals, basis, kernel):
    density = lax.dot_general(orbitals, orbitals, (((1,), (1,)), ((), ())), preferred_element_type=jnp.float32)
    weighted = (density * kernel.astype(jnp.float32)).astype(jnp.bfloat16)
    applied = jnp.dot(weighted, basis, preferred_element_type=jnp.float32).astype(jnp.bfloat16)
    return lax.dot_general(basis, applied, (((0,), (0,)), ((), ())), preferred_element_type=jnp.float32)
```

```python
import functools

import jax
import jax.numpy as jnp
from jax import lax
from jax.experimental import pallas as pl
from jax.experimental.pallas import tpu as pltpu
from jax.sharding import PartitionSpec as P

QUAD = 4
F32, BF16 = jnp.float32, jnp.bfloat16


def dot(a, b, ca, cb):
    return lax.dot_general(a, b, (((ca,), (cb,)), ((), ())), preferred_element_type=F32)


def call(body, out_shape, args, flops, scalars=1, scratch=()):
    size = sum(a.size * a.dtype.itemsize for a in args) + sum(
        o.size * o.dtype.itemsize for o in out_shape
    )
    held = size + sum(s.shape[0] * s.shape[1] * 4 for s in scratch)
    in_specs = [pl.BlockSpec(memory_space=pltpu.SMEM)] * scalars
    in_specs += [pl.BlockSpec(memory_space=pltpu.VMEM)] * (len(args) - scalars)
    return pl.pallas_call(
        body,
        out_shape=list(out_shape),
        in_specs=in_specs,
        out_specs=[pl.BlockSpec(memory_space=pltpu.VMEM)] * len(out_shape),
        scratch_shapes=list(scratch),
        cost_estimate=pl.CostEstimate(flops=flops, bytes_accessed=size, transcendentals=0),
        compiler_params=pltpu.CompilerParams(vmem_limit_bytes=held + (16 << 20)),
    )(*args)


def pick_kernel(width, me_ref, b0, b1, b2, b3, x_ref):
    place = me_ref[0] % QUAD
    columns, share = b0.shape[1], x_ref.shape[1]
    k = lax.broadcasted_iota(jnp.int32, (columns, share), 0)
    m = lax.broadcasted_iota(jnp.int32, (columns, share), 1)
    chosen = (m // width) * (QUAD * width) + place * width + m % width
    picker = (k == chosen).astype(F32).astype(BF16)
    rows = b0.shape[0]
    for r, b in enumerate((b0, b1, b2, b3)):
        x_ref[r * rows : (r + 1) * rows, :] = dot(b[...], picker, 1, 0).astype(BF16)


def main_kernel(order, width, me_ref, *refs):
    nz = len(order)
    o, k, b = refs[0:4], refs[4:8], refs[8:12]
    x = refs[12 : 12 + nz]
    own_ref, outs, total = refs[12 + nz], refs[13 + nz : 12 + 2 * nz], refs[12 + 2 * nz]
    rows = k[0].shape[0]
    me = me_ref[0]
    zi, place = me // QUAD, me % QUAD
    o_rows = jnp.concatenate([r[0:rows, :] for r in o], axis=0)
    acc = None
    for i, m in enumerate(order):
        for pair in (0, 2):
            o_cols = jnp.concatenate([o[pair + c][i * rows : (i + 1) * rows, :] for c in (0, 1)], axis=0)
            density = dot(o_rows, o_cols, 1, 1)
            at = [
                pl.multiple_of(((zi ^ m) * QUAD + (place ^ (pair + c))) * rows, rows) for c in (0, 1)
            ]
            k_block = jnp.concatenate(
                [jnp.concatenate([kr[:, pl.ds(a, rows)] for a in at], axis=1) for kr in k], axis=0
            )
            weighted = (density * k_block.astype(F32)).astype(BF16)
            term = dot(weighted, x[i][pair * rows : (pair + 2) * rows, :], 1, 0)
            acc = term if acc is None else acc + term
    applied = acc.astype(BF16)
    b_all = jnp.concatenate([r[...] for r in b], axis=0)
    total[...] = dot(applied, b_all, 0, 0)
    for m in range(nz):
        part = total[pl.ds(pl.multiple_of((zi ^ m) * width, width), width), :]
        if m == 0:
            own_ref[...] = part
        else:
            outs[m - 1][...] = part.astype(BF16)


def shards(n, orbitals, basis, kernel):
    nz = n // QUAD
    me = lax.axis_index("row")
    where = jnp.full((1,), me, jnp.int32)
    rows, columns = basis.shape
    width = columns // n

    def swap(a, bit):
        return lax.ppermute(a, "row", [(i, i ^ bit) for i in range(n)])

    def along_z(a):
        held, order, step = [a], [0], nz // 2
        while step:
            held = held + [swap(h, QUAD * step) for h in held]
            order = order + [m + step for m in order]
            step //= 2
        return held, order

    b_y, b_c = swap(basis, 2), swap(basis, 1)
    b_yc = swap(b_y, 1)
    bs = (basis, b_c, b_y, b_yc)
    (x,) = call(
        functools.partial(pick_kernel, width),
        [jax.ShapeDtypeStruct((QUAD * rows, columns // QUAD), BF16)],
        (where, *bs),
        2 * QUAD * rows * columns * columns // QUAD,
    )
    xs, order = along_z(x)
    k_y, k_c = swap(kernel, 2), swap(kernel, 1)
    k_yc = swap(k_y, 1)
    held, _ = along_z(orbitals)
    o = jnp.concatenate(held, axis=0)
    o_y, o_c = swap(o, 2), swap(o, 1)
    o_yc = swap(o_y, 1)

    points = n * rows
    flops = 2 * QUAD * rows * (points * orbitals.shape[1] + points * columns // QUAD + columns * columns // QUAD)
    parts = call(
        functools.partial(main_kernel, tuple(order), width),
        [jax.ShapeDtypeStruct((width, columns), F32 if m == 0 else BF16) for m in range(nz)],
        (where, o, o_c, o_y, o_yc, kernel, k_c, k_y, k_yc, *bs, *xs),
        flops,
        scratch=(pltpu.VMEM((columns // QUAD, columns), F32),),
    )
    total = parts[0]
    for m in range(1, nz):
        total = total + swap(parts[m], QUAD * m).astype(F32)
    return total.T


def solution(mesh):
    rows = P(("groups", "row"), None)
    return jax.shard_map(
        functools.partial(shards, mesh.shape["row"]),
        mesh=mesh,
        in_specs=(rows, rows, rows),
        out_specs=P("groups", "row"),
        check_vma=False,
    )
```

```python
import functools

import jax
import jax.numpy as jnp
from jax import lax
from jax.experimental import pallas as pl
from jax.experimental.pallas import tpu as pltpu
from jax.sharding import PartitionSpec as P

QUAD = 4
F32, BF16 = jnp.float32, jnp.bfloat16


def dot(a, b, ca, cb):
    return lax.dot_general(a, b, (((ca,), (cb,)), ((), ())), preferred_element_type=F32)


def call(body, outs, where, args, flops, scratch=()):
    size = sum(a.size * a.dtype.itemsize for a in (*args, *outs))
    held = size + sum(s.shape[0] * s.shape[1] * 4 for s in scratch)
    vmem = pl.BlockSpec(memory_space=pltpu.VMEM)
    return pl.pallas_call(
        body,
        out_shape=list(outs),
        in_specs=[pl.BlockSpec(memory_space=pltpu.SMEM)] + [vmem] * len(args),
        out_specs=[vmem] * len(outs),
        scratch_shapes=list(scratch),
        cost_estimate=pl.CostEstimate(flops=flops, bytes_accessed=size, transcendentals=0),
        compiler_params=pltpu.CompilerParams(vmem_limit_bytes=held + (16 << 20)),
    )(where, *args)


def part_kernel(me_ref, k_ref, keep_ref, send_ref):
    core, block = me_ref[0] % 2, k_ref.shape[0]
    for j in range(keep_ref.shape[1] // block):
        for ref, c in ((keep_ref, core), (send_ref, 1 - core)):
            at = pl.multiple_of((2 * j + c) * block, block)
            ref[:, j * block : (j + 1) * block] = k_ref[:, pl.ds(at, block)]


def pick_kernel(width, me_ref, own_ref, y_ref, x_ref):
    place = me_ref[0] % QUAD
    rows, columns = own_ref.shape
    share = columns // QUAD
    k = lax.broadcasted_iota(jnp.int32, (columns, share), 0)
    m = lax.broadcasted_iota(jnp.int32, (columns, share), 1)
    for c in (0, 1):
        chosen = (m // width) * (QUAD * width) + (place ^ c) * width + m % width
        picker = (k == chosen).astype(F32).astype(BF16)
        for s, b in enumerate((own_ref, y_ref)):
            x_ref[s * rows : (s + 1) * rows, c * share : (c + 1) * share] = dot(b[...], picker, 1, 0).astype(BF16)


def apply_kernel(order, me_ref, near, far, near_y, far_y, oc_ref, oyc_ref, *refs):
    nz = len(order)
    k, x, (keep_ref, send_ref) = refs[0:4], refs[4 : 4 + nz], refs[4 + nz :]
    rows = k[0].shape[0]
    zi, y = me_ref[0] // QUAD, (me_ref[0] // 2) % 2
    o_rows = jnp.concatenate([r[0:rows, :] for r in (near, oc_ref, near_y, oyc_ref)], axis=0)
    acc = None
    for i, m in enumerate(order):
        held, at = ((near, near_y), i * rows) if i * rows < near.shape[0] else ((far, far_y), i * rows - near.shape[0])
        o_cols = jnp.concatenate([r[at : at + rows, :] for r in held], axis=0)
        density = dot(o_rows, o_cols, 1, 1)
        at = [pl.multiple_of((2 * (zi ^ m) + (y ^ s)) * rows, rows) for s in (0, 1)]
        k_block = jnp.concatenate(
            [jnp.concatenate([kr[:, pl.ds(a, rows)] for a in at], axis=1) for kr in k], axis=0
        )
        weighted = (density * k_block.astype(F32)).astype(BF16)
        term = dot(weighted, x[i][...], 1, 0)
        acc = term if acc is None else acc + term
    share = acc.shape[1] // 2
    keep_ref[...] = acc[:, :share]
    for r in range(QUAD):
        send_ref[(r ^ 1) * rows : ((r ^ 1) + 1) * rows, :] = acc[r * rows : (r + 1) * rows, share:]


def project_kernel(width, me_ref, keep_ref, came_ref, b0, b1, b2, b3, *refs):
    own_ref, outs, total = refs[0], refs[1:-1], refs[-1]
    zi = me_ref[0] // QUAD
    applied = (keep_ref[...] + came_ref[...]).astype(BF16)
    b_all = jnp.concatenate([r[...] for r in (b0, b1, b2, b3)], axis=0)
    total[...] = dot(applied, b_all, 0, 0)
    for m in range(len(outs) + 1):
        part = total[pl.ds(pl.multiple_of((zi ^ m) * width, width), width), :]
        if m == 0:
            own_ref[...] = part
        else:
            outs[m - 1][...] = part.astype(BF16)


def shards(n, orbitals, basis, kernel):
    nz = n // QUAD
    where = jnp.full((1,), lax.axis_index("row"), jnp.int32)
    rows, columns = basis.shape
    width, share, points = columns // n, columns // QUAD, n * rows

    def swap(a, bit):
        return lax.ppermute(a, "row", [(i, i ^ bit) for i in range(n)])

    def after(a, *earlier):
        return lax.optimization_barrier((a, *earlier))[0]

    order, step = [0], nz // 2
    while step:
        order, step = order + [m + step for m in order], step // 2

    def first_hops(a):
        return {m: swap(a, QUAD * m) for m in order if m and m & (m - 1) == 0}

    def other_hops(a, hops):
        held = {0: a, **hops}
        for m in order:
            if m not in held:
                low = m & -m
                held[m] = swap(held[m ^ low], QUAD * low)
        return [held[m] for m in order]

    barrier = lax.optimization_barrier
    half = jax.ShapeDtypeStruct((rows, points // 2), BF16)
    k_keep, k_send = call(part_kernel, (half, half), where, (kernel,), 0)
    b_y, k_c = swap(basis, 2), swap(k_send, 1)
    o_hops = first_hops(orbitals)
    b_y, k_c, k_keep = barrier((b_y, k_c, k_keep))
    (x,) = call(
        functools.partial(pick_kernel, width),
        (jax.ShapeDtypeStruct((2 * rows, 2 * share), BF16),),
        where,
        (basis, b_y),
        8 * rows * columns * share,
    )
    near = jnp.concatenate([orbitals, *o_hops.values()], axis=0)
    k_y, near_y = swap(k_keep, 2), swap(near, 2)
    o_c, b_c = swap(orbitals, 1), swap(basis, 1)
    x_hops = first_hops(x)
    far = jnp.concatenate([a for m, a in zip(order, other_hops(orbitals, o_hops)) if m and m not in o_hops], axis=0)
    far, k_y, near_y, o_c, b_c, *x_first = barrier((far, k_y, near_y, o_c, b_c, *x_hops.values()))
    k_yc, far_y = swap(k_c, 2), swap(far, 2)
    xs = other_hops(x, dict(zip(x_hops, x_first)))
    o_yc, b_yc = swap(near_y[:rows], 1), swap(b_y, 1)
    places = [0, *o_hops, *(m for m in order if m and m not in o_hops)]
    xs = [xs[order.index(m)] for m in places]
    block = jax.ShapeDtypeStruct((QUAD * rows, share), F32)
    keep, send = call(
        functools.partial(apply_kernel, tuple(places)),
        (block, block),
        where,
        (near, far, near_y, far_y, o_c, o_yc, k_keep, k_c, k_y, k_yc, *xs),
        QUAD * rows * points * (orbitals.shape[1] + 2 * share),
    )
    parts = call(
        functools.partial(project_kernel, width),
        [jax.ShapeDtypeStruct((width, columns), BF16 if m else F32) for m in range(nz)],
        where,
        (keep, swap(send, 1), basis, b_c, b_y, b_yc),
        2 * QUAD * rows * share * columns,
        scratch=(pltpu.VMEM((share, columns), F32),),
    )
    total = parts[0]
    for m in range(1, nz):
        total = total + swap(parts[m], QUAD * m).astype(F32)
    return total.T


def solution(mesh):
    rows = P(("groups", "row"), None)
    return jax.shard_map(
        functools.partial(shards, mesh.shape["row"]),
        mesh=mesh,
        in_specs=(rows, rows, rows),
        out_specs=P("groups", "row"),
        check_vma=False,
    )
```

```python
import functools

import jax
import jax.numpy as jnp
from jax import lax
from jax.experimental import pallas as pl
from jax.experimental.pallas import tpu as pltpu
from jax.sharding import PartitionSpec as P

QUAD = 4
F32, BF16 = jnp.float32, jnp.bfloat16


def dot(a, b, ca, cb):
    return lax.dot_general(a, b, (((ca,), (cb,)), ((), ())), preferred_element_type=F32)


def call(body, outs, where, args, flops, scratch=()):
    size = sum(a.size * a.dtype.itemsize for a in (*args, *outs))
    held = size + sum(s.shape[0] * s.shape[1] * 4 for s in scratch)
    vmem = pl.BlockSpec(memory_space=pltpu.VMEM)
    return pl.pallas_call(
        body,
        out_shape=list(outs),
        in_specs=[pl.BlockSpec(memory_space=pltpu.SMEM)] + [vmem] * len(args),
        out_specs=[vmem] * len(outs),
        scratch_shapes=list(scratch),
        cost_estimate=pl.CostEstimate(flops=flops, bytes_accessed=size, transcendentals=0),
        compiler_params=pltpu.CompilerParams(vmem_limit_bytes=held + (16 << 20)),
    )(where, *args)


def part_kernel(me_ref, k_ref, keep_ref, send_ref):
    core, block = me_ref[0] % 2, k_ref.shape[0]
    for j in range(keep_ref.shape[1] // block):
        for ref, c in ((keep_ref, core), (send_ref, 1 - core)):
            at = pl.multiple_of((2 * j + c) * block, block)
            ref[:, j * block : (j + 1) * block] = k_ref[:, pl.ds(at, block)]


def pick_kernel(width, me_ref, own_ref, y_ref, x_ref):
    place = me_ref[0] % QUAD
    rows, columns = own_ref.shape
    share = columns // QUAD
    k = lax.broadcasted_iota(jnp.int32, (columns, share), 0)
    m = lax.broadcasted_iota(jnp.int32, (columns, share), 1)
    for c in (0, 1):
        chosen = (m // width) * (QUAD * width) + (place ^ c) * width + m % width
        picker = (k == chosen).astype(F32).astype(BF16)
        for s, b in enumerate((own_ref, y_ref)):
            x_ref[s * rows : (s + 1) * rows, c * share : (c + 1) * share] = dot(b[...], picker, 1, 0).astype(BF16)


def apply_kernel(order, me_ref, near, far, near_y, far_y, oc_ref, oyc_ref, *refs):
    nz = len(order)
    k, x, (keep_ref, send_ref) = refs[0:4], refs[4 : 4 + nz], refs[4 + nz :]
    rows = k[0].shape[0]
    zi, y = me_ref[0] // QUAD, (me_ref[0] // 2) % 2
    o_rows = jnp.concatenate([r[0:rows, :] for r in (near, oc_ref, near_y, oyc_ref)], axis=0)
    acc = None
    for i, m in enumerate(order):
        held, at = ((near, near_y), i * rows) if i * rows < near.shape[0] else ((far, far_y), i * rows - near.shape[0])
        o_cols = jnp.concatenate([r[at : at + rows, :] for r in held], axis=0)
        density = dot(o_rows, o_cols, 1, 1)
        at = [pl.multiple_of((2 * (zi ^ m) + (y ^ s)) * rows, rows) for s in (0, 1)]
        k_block = jnp.concatenate(
            [jnp.concatenate([kr[:, pl.ds(a, rows)] for a in at], axis=1) for kr in k], axis=0
        )
        weighted = (density * k_block.astype(F32)).astype(BF16)
        term = dot(weighted, x[i][...], 1, 0)
        acc = term if acc is None else acc + term
    share = acc.shape[1] // 2
    keep_ref[...] = acc[:, :share]
    for r in range(QUAD):
        send_ref[(r ^ 1) * rows : ((r ^ 1) + 1) * rows, :] = acc[r * rows : (r + 1) * rows, share:].astype(BF16)


def project_kernel(width, me_ref, keep_ref, came_ref, b0, b1, b2, b3, *refs):
    own_ref, outs, total = refs[0], refs[1:-1], refs[-1]
    zi = me_ref[0] // QUAD
    applied = (keep_ref[...] + came_ref[...].astype(F32)).astype(BF16)
    b_all = jnp.concatenate([r[...] for r in (b0, b1, b2, b3)], axis=0)
    total[...] = dot(applied, b_all, 0, 0)
    for m in range(len(outs) + 1):
        part = total[pl.ds(pl.multiple_of((zi ^ m) * width, width), width), :]
        if m == 0:
            own_ref[...] = part
        else:
            outs[m - 1][...] = part.astype(BF16)


def shards(n, orbitals, basis, kernel):
    nz = n // QUAD
    where = jnp.full((1,), lax.axis_index("row"), jnp.int32)
    rows, columns = basis.shape
    width, share, points = columns // n, columns // QUAD, n * rows

    def swap(a, bit):
        return lax.ppermute(a, "row", [(i, i ^ bit) for i in range(n)])

    def after(a, *earlier):
        return lax.optimization_barrier((a, *earlier))[0]

    order, step = [0], nz // 2
    while step:
        order, step = order + [m + step for m in order], step // 2

    def first_hops(a):
        return {m: swap(a, QUAD * m) for m in order if m and m & (m - 1) == 0}

    def other_hops(a, hops):
        held = {0: a, **hops}
        for m in order:
            if m not in held:
                low = m & -m
                held[m] = swap(held[m ^ low], QUAD * low)
        return [held[m] for m in order]

    barrier = lax.optimization_barrier
    half = jax.ShapeDtypeStruct((rows, points // 2), BF16)
    k_keep, k_send = call(part_kernel, (half, half), where, (kernel,), 0)
    b_y, k_c = swap(basis, 2), swap(k_send, 1)
    o_hops = first_hops(orbitals)
    b_y, k_c, k_keep = barrier((b_y, k_c, k_keep))
    (x,) = call(
        functools.partial(pick_kernel, width),
        (jax.ShapeDtypeStruct((2 * rows, 2 * share), BF16),),
        where,
        (basis, b_y),
        8 * rows * columns * share,
    )
    near = jnp.concatenate([orbitals, *o_hops.values()], axis=0)
    k_y, near_y = swap(k_keep, 2), swap(near, 2)
    o_c, b_c = swap(orbitals, 1), swap(basis, 1)
    x_hops = first_hops(x)
    far = jnp.concatenate([a for m, a in zip(order, other_hops(orbitals, o_hops)) if m and m not in o_hops], axis=0)
    b_yc = swap(b_y, 1)
    k_y, near_y, o_c, b_c, b_yc, *x_first = barrier((k_y, near_y, o_c, b_c, b_yc, *x_hops.values()))
    k_yc, far_y = swap(k_c, 2), swap(far, 2)
    xs = other_hops(x, dict(zip(x_hops, x_first)))
    o_yc = swap(near_y[:rows], 1)
    places = [0, *o_hops, *(m for m in order if m and m not in o_hops)]
    xs = [xs[order.index(m)] for m in places]
    kept = jax.ShapeDtypeStruct((QUAD * rows, share), F32)
    sent = jax.ShapeDtypeStruct((QUAD * rows, share), BF16)
    keep, send = call(
        functools.partial(apply_kernel, tuple(places)),
        (kept, sent),
        where,
        (near, far, near_y, far_y, o_c, o_yc, k_keep, k_c, k_y, k_yc, *xs),
        QUAD * rows * points * (orbitals.shape[1] + 2 * share),
    )
    parts = call(
        functools.partial(project_kernel, width),
        [jax.ShapeDtypeStruct((width, columns), BF16 if m else F32) for m in range(nz)],
        where,
        (keep, swap(send, 1), basis, b_c, b_y, b_yc),
        2 * QUAD * rows * share * columns,
        scratch=(pltpu.VMEM((share, columns), F32),),
    )
    total = parts[0]
    for m in range(nz - 1, 0, -1):
        total = total + swap(parts[m], QUAD * m).astype(F32)
    return total.T


def solution(mesh):
    rows = P(("groups", "row"), None)
    return jax.shard_map(
        functools.partial(shards, mesh.shape["row"]),
        mesh=mesh,
        in_specs=(rows, rows, rows),
        out_specs=P("groups", "row"),
        check_vma=False,
    )
```

```python
import functools

import jax
import jax.numpy as jnp
from jax import lax
from jax.experimental import pallas as pl
from jax.experimental.pallas import tpu as pltpu
from jax.sharding import PartitionSpec as P

QUAD = 4
F32, BF16 = jnp.float32, jnp.bfloat16


def dot(a, b, ca, cb):
    return lax.dot_general(a, b, (((ca,), (cb,)), ((), ())), preferred_element_type=F32)


def call(body, outs, where, args, flops, scratch=()):
    size = sum(a.size * a.dtype.itemsize for a in (*args, *outs))
    held = size + sum(s.shape[0] * s.shape[1] * 4 for s in scratch)
    vmem = pl.BlockSpec(memory_space=pltpu.VMEM)
    return pl.pallas_call(
        body,
        out_shape=list(outs),
        in_specs=[pl.BlockSpec(memory_space=pltpu.SMEM)] + [vmem] * len(args),
        out_specs=[vmem] * len(outs),
        scratch_shapes=list(scratch),
        cost_estimate=pl.CostEstimate(flops=flops, bytes_accessed=size, transcendentals=0),
        compiler_params=pltpu.CompilerParams(vmem_limit_bytes=held + (16 << 20)),
    )(where, *args)


def part_kernel(me_ref, k_ref, keep_ref, send_ref):
    core, block = me_ref[0] % 2, k_ref.shape[0]
    for j in range(keep_ref.shape[1] // block):
        for ref, c in ((keep_ref, core), (send_ref, 1 - core)):
            at = pl.multiple_of((2 * j + c) * block, block)
            ref[:, j * block : (j + 1) * block] = k_ref[:, pl.ds(at, block)]


def pick_kernel(width, me_ref, own_ref, y_ref, x_ref):
    place = me_ref[0] % QUAD
    rows, columns = own_ref.shape
    share = columns // QUAD
    k = lax.broadcasted_iota(jnp.int32, (columns, share), 0)
    m = lax.broadcasted_iota(jnp.int32, (columns, share), 1)
    for c in (0, 1):
        chosen = (m // width) * (QUAD * width) + (place ^ c) * width + m % width
        picker = (k == chosen).astype(F32).astype(BF16)
        for s, b in enumerate((own_ref, y_ref)):
            x_ref[s * rows : (s + 1) * rows, c * share : (c + 1) * share] = dot(b[...], picker, 1, 0).astype(BF16)


def weigh(o_rows, o_cols, ks, me, m):
    rows = o_cols[0].shape[0]
    density = dot(o_rows, jnp.concatenate(o_cols, axis=0), 1, 1)
    at = [pl.multiple_of((2 * (me // QUAD ^ m) + (me // 2 % 2 ^ s)) * rows, rows) for s in (0, 1)]
    k_block = jnp.concatenate(
        [jnp.concatenate([kr[:, pl.ds(a, rows)] for a in at], axis=1) for kr in ks], axis=0
    )
    return (density * k_block.astype(F32)).astype(BF16)


def early_kernel(planes, me_ref, near, near_y, oc_ref, k_keep, k_c, k_y, *refs):
    rows = oc_ref.shape[0]
    o_rows = jnp.concatenate([near[0:rows, :], oc_ref[...], near_y[0:rows, :]], axis=0)
    acc = None
    for i, m in enumerate(planes):
        o_cols = [r[i * rows : (i + 1) * rows, :] for r in (near, near_y)]
        term = dot(weigh(o_rows, o_cols, (k_keep, k_c, k_y), me_ref[0], m), refs[i][...], 1, 0)
        acc = term if acc is None else acc + term
    refs[-1][...] = acc


def apply_kernel(planes, me_ref, early, near, far, near_y, far_y, oc_ref, oyc_ref, *refs):
    nz = len(planes)
    k, x, (keep_ref, send_ref) = refs[0:4], refs[4 : 4 + nz], refs[4 + nz :]
    rows = oc_ref.shape[0]
    o_rows = jnp.concatenate([near[0:rows, :], oc_ref[...], near_y[0:rows, :]], axis=0)
    top, last = early[...], None
    for i, m in enumerate(planes):
        late = i * rows >= near.shape[0]
        held, at = ((far, far_y), i * rows - near.shape[0]) if late else ((near, near_y), i * rows)
        o_cols = [r[at : at + rows, :] for r in held]
        if late:
            top += dot(weigh(o_rows, o_cols, k[:3], me_ref[0], m), x[i][...], 1, 0)
        term = dot(weigh(oyc_ref[...], o_cols, k[3:], me_ref[0], m), x[i][...], 1, 0)
        last = term if last is None else last + term
    share = top.shape[1] // 2
    for r in range(QUAD):
        part = last if r == QUAD - 1 else top[r * rows : (r + 1) * rows, :]
        keep_ref[r * rows : (r + 1) * rows, :] = part[:, :share]
        send_ref[(r ^ 1) * rows : ((r ^ 1) + 1) * rows, :] = part[:, share:]


def project_kernel(width, me_ref, keep_ref, came_ref, b0, b1, b2, b3, *refs):
    own_ref, outs, total = refs[0], refs[1:-1], refs[-1]
    zi = me_ref[0] // QUAD
    applied = (keep_ref[...] + came_ref[...]).astype(BF16)
    b_all = jnp.concatenate([r[...] for r in (b0, b1, b2, b3)], axis=0)
    total[...] = dot(applied, b_all, 0, 0)
    for m in range(len(outs) + 1):
        part = total[pl.ds(pl.multiple_of((zi ^ m) * width, width), width), :]
        if m == 0:
            own_ref[...] = part
        else:
            outs[m - 1][...] = part.astype(BF16)


def shards(n, orbitals, basis, kernel):
    nz = n // QUAD
    where = jnp.full((1,), lax.axis_index("row"), jnp.int32)
    rows, columns = basis.shape
    width, share, points = columns // n, columns // QUAD, n * rows

    def swap(a, bit):
        return lax.ppermute(a, "row", [(i, i ^ bit) for i in range(n)])

    def after(a, *earlier):
        return lax.optimization_barrier((a, *earlier))[0]

    order, step = [0], nz // 2
    while step:
        order, step = order + [m + step for m in order], step // 2

    def first_hops(a):
        return {m: swap(a, QUAD * m) for m in order if m and m & (m - 1) == 0}

    def other_hops(a, hops):
        held = {0: a, **hops}
        for m in order:
            if m not in held:
                low = m & -m
                held[m] = swap(held[m ^ low], QUAD * low)
        return [held[m] for m in order]

    barrier = lax.optimization_barrier
    half = jax.ShapeDtypeStruct((rows, points // 2), BF16)
    k_keep, k_send = call(part_kernel, (half, half), where, (kernel,), 0)
    b_y, k_c = swap(basis, 2), swap(k_send, 1)
    o_hops = first_hops(orbitals)
    b_y, k_c, k_keep = barrier((b_y, k_c, k_keep))
    (x,) = call(
        functools.partial(pick_kernel, width),
        (jax.ShapeDtypeStruct((2 * rows, 2 * share), BF16),),
        where,
        (basis, b_y),
        8 * rows * columns * share,
    )
    near = jnp.concatenate([orbitals, *o_hops.values()], axis=0)
    k_y, near_y = swap(k_keep, 2), swap(near, 2)
    o_c, b_c = swap(orbitals, 1), swap(basis, 1)
    x_hops = first_hops(x)
    far = jnp.concatenate([a for m, a in zip(order, other_hops(orbitals, o_hops)) if m and m not in o_hops], axis=0)
    b_yc = swap(b_y, 1)
    k_y, near_y, o_c, b_c, b_yc, *x_first = barrier((k_y, near_y, o_c, b_c, b_yc, *x_hops.values()))
    k_yc, far_y = swap(k_c, 2), swap(far, 2)
    xs = other_hops(x, dict(zip(x_hops, x_first)))
    o_yc = swap(near_y[:rows], 1)
    places = [0, *o_hops, *(m for m in order if m and m not in o_hops)]
    xs = [xs[order.index(m)] for m in places]
    block = jax.ShapeDtypeStruct((QUAD * rows, share), F32)
    n_near = 1 + len(o_hops)
    (early,) = call(
        functools.partial(early_kernel, tuple(places[:n_near])),
        (jax.ShapeDtypeStruct((3 * rows, 2 * share), F32),),
        where,
        (near, near_y, o_c, k_keep, k_c, k_y, *xs[:n_near]),
        12 * rows * n_near * rows * (orbitals.shape[1] + 2 * share),
    )
    keep, send = call(
        functools.partial(apply_kernel, tuple(places)),
        (block, block),
        where,
        (early, near, far, near_y, far_y, o_c, o_yc, k_keep, k_c, k_y, k_yc, *xs),
        QUAD * rows * points * (orbitals.shape[1] + 2 * share) // 2,
    )
    parts = call(
        functools.partial(project_kernel, width),
        [jax.ShapeDtypeStruct((width, columns), BF16 if m else F32) for m in range(nz)],
        where,
        (keep, swap(send, 1), basis, b_c, b_y, b_yc),
        2 * QUAD * rows * share * columns,
        scratch=(pltpu.VMEM((share, columns), F32),),
    )
    total = parts[0]
    for m in range(nz - 1, 0, -1):
        total = total + swap(parts[m], QUAD * m).astype(F32)
    return total.T


def solution(mesh):
    rows = P(("groups", "row"), None)
    return jax.shard_map(
        functools.partial(shards, mesh.shape["row"]),
        mesh=mesh,
        in_specs=(rows, rows, rows),
        out_specs=P("groups", "row"),
        check_vma=False,
    )
```

```python
import functools

import jax
import jax.numpy as jnp
from jax import lax
from jax.experimental import pallas as pl
from jax.experimental.pallas import tpu as pltpu
from jax.sharding import PartitionSpec as P

QUAD = 4
F32, BF16 = jnp.float32, jnp.bfloat16


def dot(a, b, ca, cb):
    return lax.dot_general(a, b, (((ca,), (cb,)), ((), ())), preferred_element_type=F32)


def call(body, outs, where, args, flops, scratch=()):
    size = sum(a.size * a.dtype.itemsize for a in (*args, *outs))
    held = size + sum(s.shape[0] * s.shape[1] * 4 for s in scratch)
    vmem = pl.BlockSpec(memory_space=pltpu.VMEM)
    return pl.pallas_call(
        body,
        out_shape=list(outs),
        in_specs=[pl.BlockSpec(memory_space=pltpu.SMEM)] + [vmem] * len(args),
        out_specs=[vmem] * len(outs),
        scratch_shapes=list(scratch),
        cost_estimate=pl.CostEstimate(flops=flops, bytes_accessed=size, transcendentals=0),
        compiler_params=pltpu.CompilerParams(vmem_limit_bytes=held + (16 << 20)),
    )(where, *args)


def part_kernel(me_ref, k_ref, keep_ref, send_ref):
    core, block = me_ref[0] % 2, k_ref.shape[0]
    for j in range(keep_ref.shape[1] // block):
        for ref, c in ((keep_ref, core), (send_ref, 1 - core)):
            at = pl.multiple_of((2 * j + c) * block, block)
            ref[:, j * block : (j + 1) * block] = k_ref[:, pl.ds(at, block)]


def pick_kernel(width, me_ref, own_ref, y_ref, x_ref):
    place = me_ref[0] % QUAD
    rows, columns = own_ref.shape
    share = columns // QUAD
    k = lax.broadcasted_iota(jnp.int32, (columns, share), 0)
    m = lax.broadcasted_iota(jnp.int32, (columns, share), 1)
    for c in (0, 1):
        chosen = (m // width) * (QUAD * width) + (place ^ c) * width + m % width
        picker = (k == chosen).astype(F32).astype(BF16)
        for s, b in enumerate((own_ref, y_ref)):
            x_ref[s * rows : (s + 1) * rows, c * share : (c + 1) * share] = dot(b[...], picker, 1, 0).astype(BF16)


def weigh(o_rows, o_cols, ks, me, m):
    rows = o_cols[0].shape[0]
    density = dot(o_rows, jnp.concatenate(o_cols, axis=0), 1, 1)
    at = [pl.multiple_of((2 * (me // QUAD ^ m) + (me // 2 % 2 ^ s)) * rows, rows) for s in (0, 1)]
    k_block = jnp.concatenate(
        [jnp.concatenate([kr[:, pl.ds(a, rows)] for a in at], axis=1) for kr in ks], axis=0
    )
    return (density * k_block.astype(F32)).astype(BF16)


def early_kernel(planes, me_ref, near, near_y, oc_ref, k_keep, k_c, k_y, *refs):
    rows = oc_ref.shape[0]
    o_rows = jnp.concatenate([near[0:rows, :], oc_ref[...], near_y[0:rows, :]], axis=0)
    acc = None
    for i, m in enumerate(planes):
        o_cols = [r[i * rows : (i + 1) * rows, :] for r in (near, near_y)]
        term = dot(weigh(o_rows, o_cols, (k_keep, k_c, k_y), me_ref[0], m), refs[i][...], 1, 0)
        acc = term if acc is None else acc + term
    refs[-1][...] = acc


def apply_kernel(planes, me_ref, early, near, far, near_y, far_y, oc_ref, oyc_ref, *refs):
    nz = len(planes)
    k, x, (keep_ref, send_ref) = refs[0:4], refs[4 : 4 + nz], refs[4 + nz :]
    rows = oc_ref.shape[0]
    o_rows = jnp.concatenate([near[0:rows, :], oc_ref[...], near_y[0:rows, :]], axis=0)
    top, last = early[...], None
    for i, m in enumerate(planes):
        late = i * rows >= near.shape[0]
        held, at = ((far, far_y), i * rows - near.shape[0]) if late else ((near, near_y), i * rows)
        o_cols = [r[at : at + rows, :] for r in held]
        if late:
            top += dot(weigh(o_rows, o_cols, k[:3], me_ref[0], m), x[i][...], 1, 0)
        term = dot(weigh(oyc_ref[...], o_cols, k[3:], me_ref[0], m), x[i][...], 1, 0)
        last = term if last is None else last + term
    share = top.shape[1] // 2
    for r in range(QUAD):
        part = last if r == QUAD - 1 else top[r * rows : (r + 1) * rows, :]
        keep_ref[r * rows : (r + 1) * rows, :] = part[:, :share]
        send_ref[(r ^ 1) * rows : ((r ^ 1) + 1) * rows, :] = part[:, share:]


def project_kernel(width, me_ref, keep_ref, came_ref, b0, b1, b2, b3, *refs):
    own_ref, outs, total = refs[0], refs[1:-1], refs[-1]
    zi = me_ref[0] // QUAD
    applied = (keep_ref[...] + came_ref[...]).astype(BF16)
    b_all = jnp.concatenate([r[...] for r in (b0, b1, b2, b3)], axis=0)
    total[...] = dot(applied, b_all, 0, 0)
    for m in range(len(outs) + 1):
        part = total[pl.ds(pl.multiple_of((zi ^ m) * width, width), width), :]
        if m == 0:
            own_ref[...] = part
        else:
            outs[m - 1][...] = part.astype(BF16)


def shards(n, orbitals, basis, kernel):
    nz = n // QUAD
    where = jnp.full((1,), lax.axis_index("row"), jnp.int32)
    rows, columns = basis.shape
    width, share, points = columns // n, columns // QUAD, n * rows

    def swap(a, bit):
        return lax.ppermute(a, "row", [(i, i ^ bit) for i in range(n)])

    def after(a, *earlier):
        return lax.optimization_barrier((a, *earlier))[0]

    order, step = [0], nz // 2
    while step:
        order, step = order + [m + step for m in order], step // 2

    def first_hops(a):
        return {m: swap(a, QUAD * m) for m in order if m and m & (m - 1) == 0}

    def other_hops(a, hops):
        held = {0: a, **hops}
        for m in order:
            if m not in held:
                low = m & -m
                held[m] = swap(held[m ^ low], QUAD * low)
        return [held[m] for m in order]

    barrier = lax.optimization_barrier
    half = jax.ShapeDtypeStruct((rows, points // 2), BF16)
    k_keep, k_send = call(part_kernel, (half, half), where, (kernel,), 0)
    b_y, k_c = swap(basis, 2), swap(k_send, 1)
    o_hops = first_hops(orbitals)
    b_y, k_c, k_keep = barrier((b_y, k_c, k_keep))
    (x,) = call(
        functools.partial(pick_kernel, width),
        (jax.ShapeDtypeStruct((2 * rows, 2 * share), BF16),),
        where,
        (basis, b_y),
        8 * rows * columns * share,
    )
    near = jnp.concatenate([orbitals, *o_hops.values()], axis=0)
    k_y, near_y = swap(k_keep, 2), swap(near, 2)
    o_c, b_c = swap(orbitals, 1), swap(basis, 1)
    x_hops = first_hops(x)
    far = jnp.concatenate([a for m, a in zip(order, other_hops(orbitals, o_hops)) if m and m not in o_hops], axis=0)
    b_yc = swap(b_y, 1)
    k_y, near_y, o_c, b_c, b_yc, *x_first = barrier((k_y, near_y, o_c, b_c, b_yc, *x_hops.values()))
    k_yc, far_y = swap(k_c, 2), swap(far, 2)
    xs = other_hops(x, dict(zip(x_hops, x_first)))
    o_yc = swap(near_y[:rows], 1)
    places = [0, *o_hops, *(m for m in order if m and m not in o_hops)]
    xs = [xs[order.index(m)] for m in places]
    block = jax.ShapeDtypeStruct((QUAD * rows, share), F32)
    n_near = 1 + len(o_hops)
    (early,) = call(
        functools.partial(early_kernel, tuple(places[:n_near])),
        (jax.ShapeDtypeStruct((3 * rows, 2 * share), F32),),
        where,
        (near, near_y, o_c, k_keep, k_c, k_y, *xs[:n_near]),
        12 * rows * n_near * rows * (orbitals.shape[1] + 2 * share),
    )
    keep, send = call(
        functools.partial(apply_kernel, tuple(places)),
        (block, block),
        where,
        (early, near, far, near_y, far_y, o_c, o_yc, k_keep, k_c, k_y, k_yc, *xs),
        QUAD * rows * points * (orbitals.shape[1] + 2 * share) // 2,
    )
    parts = call(
        functools.partial(project_kernel, width),
        [jax.ShapeDtypeStruct((width, columns), BF16 if m else F32) for m in range(nz)],
        where,
        (keep, swap(send, 1), basis, b_c, b_y, b_yc),
        2 * QUAD * rows * share * columns,
        scratch=(pltpu.VMEM((share, columns), F32),),
    )
    total = parts[0]
    for m in range(1, nz):
        total = total + swap(parts[m], QUAD * m).astype(F32)
    return total.T


def solution(mesh):
    rows = P(("groups", "row"), None)
    return jax.shard_map(
        functools.partial(shards, mesh.shape["row"]),
        mesh=mesh,
        in_specs=(rows, rows, rows),
        out_specs=P("groups", "row"),
        check_vma=False,
    )
```

```python
import functools

import jax
import jax.numpy as jnp
from jax import lax
from jax.experimental import pallas as pl
from jax.experimental.pallas import tpu as pltpu
from jax.sharding import PartitionSpec as P

QUAD = 4
F32, BF16 = jnp.float32, jnp.bfloat16


def dot(a, b, ca, cb):
    return lax.dot_general(a, b, (((ca,), (cb,)), ((), ())), preferred_element_type=F32)


def call(body, outs, where, args, flops, scratch=()):
    size = sum(a.size * a.dtype.itemsize for a in (*args, *outs))
    held = size + sum(s.shape[0] * s.shape[1] * 4 for s in scratch)
    vmem = pl.BlockSpec(memory_space=pltpu.VMEM)
    return pl.pallas_call(
        body,
        out_shape=list(outs),
        in_specs=[pl.BlockSpec(memory_space=pltpu.SMEM)] + [vmem] * len(args),
        out_specs=[vmem] * len(outs),
        scratch_shapes=list(scratch),
        cost_estimate=pl.CostEstimate(flops=flops, bytes_accessed=size, transcendentals=0),
        compiler_params=pltpu.CompilerParams(vmem_limit_bytes=held + (16 << 20)),
    )(where, *args)


def part_kernel(me_ref, k_ref, keep_ref, send_ref):
    core, block = me_ref[0] % 2, k_ref.shape[0]
    for j in range(keep_ref.shape[1] // block):
        for ref, c in ((keep_ref, core), (send_ref, 1 - core)):
            at = pl.multiple_of((2 * j + c) * block, block)
            ref[:, j * block : (j + 1) * block] = k_ref[:, pl.ds(at, block)]


def pick_kernel(width, me_ref, own_ref, y_ref, x_ref):
    place = me_ref[0] % QUAD
    rows, columns = own_ref.shape
    share = columns // QUAD
    k = lax.broadcasted_iota(jnp.int32, (columns, share), 0)
    m = lax.broadcasted_iota(jnp.int32, (columns, share), 1)
    for c in (0, 1):
        chosen = (m // width) * (QUAD * width) + (place ^ c) * width + m % width
        picker = (k == chosen).astype(F32).astype(BF16)
        for s, b in enumerate((own_ref, y_ref)):
            x_ref[s * rows : (s + 1) * rows, c * share : (c + 1) * share] = dot(b[...], picker, 1, 0).astype(BF16)


def weigh(o_rows, o_cols, ks, me, m, density=None):
    rows = o_cols[0].shape[0]
    if density is None:
        density = dot(o_rows, jnp.concatenate(o_cols, axis=0), 1, 1)
    at = [pl.multiple_of((2 * (me // QUAD ^ m) + (me // 2 % 2 ^ s)) * rows, rows) for s in (0, 1)]
    k_block = jnp.concatenate(
        [jnp.concatenate([kr[:, pl.ds(a, rows)] for a in at], axis=1) for kr in ks], axis=0
    )
    return (density * k_block.astype(F32)).astype(BF16)


def early_kernel(planes, me_ref, near, near_y, oc_ref, oyc_ref, k_keep, k_c, k_y, *refs):
    rows = oc_ref.shape[0]
    o_rows = jnp.concatenate([near[0:rows, :], oc_ref[...], near_y[0:rows, :]], axis=0)
    acc = None
    for i, m in enumerate(planes):
        o_cols = [r[i * rows : (i + 1) * rows, :] for r in (near, near_y)]
        term = dot(weigh(o_rows, o_cols, (k_keep, k_c, k_y), me_ref[0], m), refs[i][...], 1, 0)
        acc = term if acc is None else acc + term
        refs[-1][:, 2 * i * rows : 2 * (i + 1) * rows] = dot(oyc_ref[...], jnp.concatenate(o_cols, axis=0), 1, 1)
    refs[-2][...] = acc


def apply_kernel(planes, me_ref, early, ready, near, far, near_y, far_y, oc_ref, oyc_ref, *refs):
    nz = len(planes)
    k, x, (keep_ref, send_ref) = refs[0:4], refs[4 : 4 + nz], refs[4 + nz :]
    rows = oc_ref.shape[0]
    o_rows = jnp.concatenate([near[0:rows, :], oc_ref[...], near_y[0:rows, :]], axis=0)
    top, last = early[...], None
    for i, m in enumerate(planes):
        late = i * rows >= near.shape[0]
        held, at = ((far, far_y), i * rows - near.shape[0]) if late else ((near, near_y), i * rows)
        o_cols = [r[at : at + rows, :] for r in held]
        if late:
            top += dot(weigh(o_rows, o_cols, k[:3], me_ref[0], m), x[i][...], 1, 0)
        known = None if late else ready[:, 2 * i * rows : 2 * (i + 1) * rows]
        term = dot(weigh(oyc_ref[...], o_cols, k[3:], me_ref[0], m, known), x[i][...], 1, 0)
        last = term if last is None else last + term
    share = top.shape[1] // 2
    for r in range(QUAD):
        part = last if r == QUAD - 1 else top[r * rows : (r + 1) * rows, :]
        keep_ref[r * rows : (r + 1) * rows, :] = part[:, :share]
        send_ref[(r ^ 1) * rows : ((r ^ 1) + 1) * rows, :] = part[:, share:]


def project_kernel(width, me_ref, keep_ref, came_ref, b0, b1, b2, b3, *refs):
    own_ref, outs, total = refs[0], refs[1:-1], refs[-1]
    zi = me_ref[0] // QUAD
    applied = (keep_ref[...] + came_ref[...]).astype(BF16)
    b_all = jnp.concatenate([r[...] for r in (b0, b1, b2, b3)], axis=0)
    total[...] = dot(applied, b_all, 0, 0)
    for m in range(len(outs) + 1):
        part = total[pl.ds(pl.multiple_of((zi ^ m) * width, width), width), :]
        if m == 0:
            own_ref[...] = part
        else:
            outs[m - 1][...] = part.astype(BF16)


def shards(n, orbitals, basis, kernel):
    nz = n // QUAD
    where = jnp.full((1,), lax.axis_index("row"), jnp.int32)
    rows, columns = basis.shape
    width, share, points = columns // n, columns // QUAD, n * rows

    def swap(a, bit):
        return lax.ppermute(a, "row", [(i, i ^ bit) for i in range(n)])

    def after(a, *earlier):
        return lax.optimization_barrier((a, *earlier))[0]

    order, step = [0], nz // 2
    while step:
        order, step = order + [m + step for m in order], step // 2

    def first_hops(a):
        return {m: swap(a, QUAD * m) for m in order if m and m & (m - 1) == 0}

    def other_hops(a, hops):
        held = {0: a, **hops}
        for m in order:
            if m not in held:
                low = m & -m
                held[m] = swap(held[m ^ low], QUAD * low)
        return [held[m] for m in order]

    barrier = lax.optimization_barrier
    half = jax.ShapeDtypeStruct((rows, points // 2), BF16)
    k_keep, k_send = call(part_kernel, (half, half), where, (kernel,), 0)
    b_y, k_c = swap(basis, 2), swap(k_send, 1)
    o_hops = first_hops(orbitals)
    b_y, k_c, k_keep = barrier((b_y, k_c, k_keep))
    (x,) = call(
        functools.partial(pick_kernel, width),
        (jax.ShapeDtypeStruct((2 * rows, 2 * share), BF16),),
        where,
        (basis, b_y),
        8 * rows * columns * share,
    )
    near = jnp.concatenate([orbitals, *o_hops.values()], axis=0)
    k_y, near_y = swap(k_keep, 2), swap(near, 2)
    o_c, b_c = swap(orbitals, 1), swap(basis, 1)
    x_hops = first_hops(x)
    far = jnp.concatenate([a for m, a in zip(order, other_hops(orbitals, o_hops)) if m and m not in o_hops], axis=0)
    b_yc = swap(b_y, 1)
    k_y, near_y, o_c, b_c, b_yc, *x_first = barrier((k_y, near_y, o_c, b_c, b_yc, *x_hops.values()))
    k_yc, far_y = swap(k_c, 2), swap(far, 2)
    xs = other_hops(x, dict(zip(x_hops, x_first)))
    o_yc = swap(near_y[:rows], 1)
    places = [0, *o_hops, *(m for m in order if m and m not in o_hops)]
    xs = [xs[order.index(m)] for m in places]
    block = jax.ShapeDtypeStruct((QUAD * rows, share), F32)
    n_near = 1 + len(o_hops)
    early, ready = call(
        functools.partial(early_kernel, tuple(places[:n_near])),
        (
            jax.ShapeDtypeStruct((3 * rows, 2 * share), F32),
            jax.ShapeDtypeStruct((rows, n_near * 2 * rows), F32),
        ),
        where,
        (near, near_y, o_c, o_yc, k_keep, k_c, k_y, *xs[:n_near]),
        12 * rows * n_near * rows * (orbitals.shape[1] + 2 * share),
    )
    keep, send = call(
        functools.partial(apply_kernel, tuple(places)),
        (block, block),
        where,
        (early, ready, near, far, near_y, far_y, o_c, o_yc, k_keep, k_c, k_y, k_yc, *xs),
        QUAD * rows * points * (orbitals.shape[1] + 2 * share) // 2,
    )
    parts = call(
        functools.partial(project_kernel, width),
        [jax.ShapeDtypeStruct((width, columns), BF16 if m else F32) for m in range(nz)],
        where,
        (keep, swap(send, 1), basis, b_c, b_y, b_yc),
        2 * QUAD * rows * share * columns,
        scratch=(pltpu.VMEM((share, columns), F32),),
    )
    total = parts[0]
    for m in range(1, nz):
        total = total + swap(parts[m], QUAD * m).astype(F32)
    return total.T


def solution(mesh):
    rows = P(("groups", "row"), None)
    return jax.shard_map(
        functools.partial(shards, mesh.shape["row"]),
        mesh=mesh,
        in_specs=(rows, rows, rows),
        out_specs=P("groups", "row"),
        check_vma=False,
    )
```

```python
import functools

import jax
import jax.numpy as jnp
from jax import lax
from jax.experimental import pallas as pl
from jax.experimental.pallas import tpu as pltpu
from jax.sharding import PartitionSpec as P

QUAD = 4
F32, BF16 = jnp.float32, jnp.bfloat16


def dot(a, b, ca, cb):
    return lax.dot_general(a, b, (((ca,), (cb,)), ((), ())), preferred_element_type=F32)


def call(body, outs, where, args, flops, scratch=()):
    size = sum(a.size * a.dtype.itemsize for a in (*args, *outs))
    held = size + sum(s.shape[0] * s.shape[1] * 4 for s in scratch)
    vmem = pl.BlockSpec(memory_space=pltpu.VMEM)
    return pl.pallas_call(
        body,
        out_shape=list(outs),
        in_specs=[pl.BlockSpec(memory_space=pltpu.SMEM)] + [vmem] * len(args),
        out_specs=[vmem] * len(outs),
        scratch_shapes=list(scratch),
        cost_estimate=pl.CostEstimate(flops=flops, bytes_accessed=size, transcendentals=0),
        compiler_params=pltpu.CompilerParams(vmem_limit_bytes=held + (16 << 20)),
    )(where, *args)


def part_kernel(me_ref, k_ref, keep_ref, send_ref):
    core, block = me_ref[0] % 2, k_ref.shape[0]
    for j in range(keep_ref.shape[1] // block):
        for ref, c in ((keep_ref, core), (send_ref, 1 - core)):
            at = pl.multiple_of((2 * j + c) * block, block)
            ref[:, j * block : (j + 1) * block] = k_ref[:, pl.ds(at, block)]


def pick_kernel(width, me_ref, own_ref, y_ref, x_ref):
    place = me_ref[0] % QUAD
    rows, columns = own_ref.shape
    share = columns // QUAD
    k = lax.broadcasted_iota(jnp.int32, (columns, share), 0)
    m = lax.broadcasted_iota(jnp.int32, (columns, share), 1)
    for c in (0, 1):
        chosen = (m // width) * (QUAD * width) + (place ^ c) * width + m % width
        picker = (k == chosen).astype(F32).astype(BF16)
        for s, b in enumerate((own_ref, y_ref)):
            x_ref[s * rows : (s + 1) * rows, c * share : (c + 1) * share] = dot(b[...], picker, 1, 0).astype(BF16)


def weigh(o_rows, o_cols, ks, me, m):
    rows = o_cols[0].shape[0]
    density = dot(o_rows, jnp.concatenate(o_cols, axis=0), 1, 1)
    at = [pl.multiple_of((2 * (me // QUAD ^ m) + (me // 2 % 2 ^ s)) * rows, rows) for s in (0, 1)]
    k_block = jnp.concatenate(
        [jnp.concatenate([kr[:, pl.ds(a, rows)] for a in at], axis=1) for kr in ks], axis=0
    )
    return (density * k_block.astype(F32)).astype(BF16)


def early_kernel(planes, me_ref, near, near_y, oc_ref, k_keep, k_c, k_y, *refs):
    rows = oc_ref.shape[0]
    o_rows = jnp.concatenate([near[0:rows, :], oc_ref[...], near_y[0:rows, :]], axis=0)
    acc = None
    for i, m in enumerate(planes):
        o_cols = [r[i * rows : (i + 1) * rows, :] for r in (near, near_y)]
        term = dot(weigh(o_rows, o_cols, (k_keep, k_c, k_y), me_ref[0], m), refs[i][...], 1, 0)
        acc = term if acc is None else acc + term
    refs[-1][...] = acc


def apply_kernel(planes, me_ref, early, near, far, near_y, far_y, oc_ref, oyc_ref, *refs):
    nz = len(planes)
    k, x, (keep_ref, send_ref) = refs[0:4], refs[4 : 4 + nz], refs[4 + nz :]
    rows = oc_ref.shape[0]
    o_rows = jnp.concatenate([near[0:rows, :], oc_ref[...], near_y[0:rows, :]], axis=0)
    top, last = early[...], None
    for i, m in enumerate(planes):
        late = i * rows >= near.shape[0]
        held, at = ((far, far_y), i * rows - near.shape[0]) if late else ((near, near_y), i * rows)
        o_cols = [r[at : at + rows, :] for r in held]
        if late:
            top += dot(weigh(o_rows, o_cols, k[:3], me_ref[0], m), x[i][...], 1, 0)
        term = dot(weigh(oyc_ref[...], o_cols, k[3:], me_ref[0], m), x[i][...], 1, 0)
        last = term if last is None else last + term
    share = top.shape[1] // 2
    for r in range(QUAD):
        part = last if r == QUAD - 1 else top[r * rows : (r + 1) * rows, :]
        keep_ref[r * rows : (r + 1) * rows, :] = part[:, :share]
        send_ref[(r ^ 1) * rows : ((r ^ 1) + 1) * rows, :] = part[:, share:]


def project_kernel(width, me_ref, keep_ref, came_ref, b0, b1, b2, b3, *refs):
    own_ref, outs, total = refs[0], refs[1:-1], refs[-1]
    zi = me_ref[0] // QUAD
    applied = (keep_ref[...] + came_ref[...]).astype(BF16)
    b_all = jnp.concatenate([r[...] for r in (b0, b1, b2, b3)], axis=0)
    total[...] = dot(applied, b_all, 0, 0)
    for m in range(len(outs) + 1):
        part = total[pl.ds(pl.multiple_of((zi ^ m) * width, width), width), :]
        if m == 0:
            own_ref[...] = part
        else:
            outs[m - 1][...] = part.astype(BF16)


def shards(n, orbitals, basis, kernel):
    nz = n // QUAD
    where = jnp.full((1,), lax.axis_index("row"), jnp.int32)
    rows, columns = basis.shape
    width, share, points = columns // n, columns // QUAD, n * rows

    def swap(a, bit):
        return lax.ppermute(a, "row", [(i, i ^ bit) for i in range(n)])

    def after(a, *earlier):
        return lax.optimization_barrier((a, *earlier))[0]

    order, step = [0], nz // 2
    while step:
        order, step = order + [m + step for m in order], step // 2

    def first_hops(a):
        return {m: swap(a, QUAD * m) for m in order if m and m & (m - 1) == 0}

    def other_hops(a, hops):
        held = {0: a, **hops}
        for m in order:
            if m not in held:
                low = m & -m
                held[m] = swap(held[m ^ low], QUAD * low)
        return [held[m] for m in order]

    barrier = lax.optimization_barrier
    half = jax.ShapeDtypeStruct((rows, points // 2), BF16)
    k_keep, k_send = call(part_kernel, (half, half), where, (kernel,), 0)
    b_y, k_c = swap(basis, 2), swap(k_send, 1)
    o_hops = first_hops(orbitals)
    b_y, k_keep = barrier((b_y, k_keep))
    (x,) = call(
        functools.partial(pick_kernel, width),
        (jax.ShapeDtypeStruct((2 * rows, 2 * share), BF16),),
        where,
        (basis, b_y),
        8 * rows * columns * share,
    )
    near = jnp.concatenate([orbitals, *o_hops.values()], axis=0)
    k_y, near_y = swap(k_keep, 2), swap(near, 2)
    o_c, b_c = swap(orbitals, 1), swap(basis, 1)
    x_hops = first_hops(x)
    far = jnp.concatenate([a for m, a in zip(order, other_hops(orbitals, o_hops)) if m and m not in o_hops], axis=0)
    b_yc = swap(b_y, 1)
    k_y, near_y, o_c, b_c, b_yc, *x_first = barrier((k_y, near_y, o_c, b_c, b_yc, *x_hops.values()))
    k_yc, far_y = swap(k_c, 2), swap(far, 2)
    xs = other_hops(x, dict(zip(x_hops, x_first)))
    o_yc = swap(near_y[:rows], 1)
    places = [0, *o_hops, *(m for m in order if m and m not in o_hops)]
    xs = [xs[order.index(m)] for m in places]
    block = jax.ShapeDtypeStruct((QUAD * rows, share), F32)
    n_near = 1 + len(o_hops)
    (early,) = call(
        functools.partial(early_kernel, tuple(places[:n_near])),
        (jax.ShapeDtypeStruct((3 * rows, 2 * share), F32),),
        where,
        (near, near_y, o_c, k_keep, k_c, k_y, *xs[:n_near]),
        12 * rows * n_near * rows * (orbitals.shape[1] + 2 * share),
    )
    keep, send = call(
        functools.partial(apply_kernel, tuple(places)),
        (block, block),
        where,
        (early, near, far, near_y, far_y, o_c, o_yc, k_keep, k_c, k_y, k_yc, *xs),
        QUAD * rows * points * (orbitals.shape[1] + 2 * share) // 2,
    )
    parts = call(
        functools.partial(project_kernel, width),
        [jax.ShapeDtypeStruct((width, columns), BF16 if m else F32) for m in range(nz)],
        where,
        (keep, swap(send, 1), basis, b_c, b_y, b_yc),
        2 * QUAD * rows * share * columns,
        scratch=(pltpu.VMEM((share, columns), F32),),
    )
    total = parts[0]
    for m in range(1, nz):
        total = total + swap(parts[m], QUAD * m).astype(F32)
    return total.T


def solution(mesh):
    rows = P(("groups", "row"), None)
    return jax.shard_map(
        functools.partial(shards, mesh.shape["row"]),
        mesh=mesh,
        in_specs=(rows, rows, rows),
        out_specs=P("groups", "row"),
        check_vma=False,
    )
```
